32 devices in a mesh: groups: 2 (over y), dp: 2 (over x), expert: 8 (over z, core).
Axes of the slice: x: 2, y: 2, z: 4, core: 2. Of those that a mesh axis runs over, the one named last changes fastest.
Arguments:
- tokens: bfloat16 [4096, 2048], P(('groups', 'dp', 'expert')), parts along dimension 0, may hold values from -6 to 6
- routes: int32 [4096, 4], P(('groups', 'dp', 'expert')), parts along dimension 0, may hold values from 0 to 7, all different within a row; in each aligned block of 128 rows (0 to 127, 128 to 255, ...) at most 128 rows name the same one
- w_gate: bfloat16 [16, 2048, 512], P(('groups', 'expert')), parts along dimension 0, may hold values from -0.125 to 0.125
- w_up: bfloat16 [16, 2048, 512], P(('groups', 'expert')), parts along dimension 0, may hold values from -0.125 to 0.125
Outputs:
- r_factor: float32 [16, 512, 512], P(('groups', 'expert'), 'dp'), parts along dimension 0
The draws below stay inside these ranges and needn't reach their ends.
There are 2 independent parts, one for each index of `groups`. The reference program is written for one: setup_inputs(seed, part) draws one part's arguments, and reference() takes and returns one part's arrays. A program takes and returns all parts, laid end to end along the dimension named above; each array names one. Nothing has to cross between parts.
Inputs may be any that keep to these rules, and one draw needn't show every extreme that they name: `routes`: each row names 4 different experts. In each aligned block of 128 rows (the tokens of one device) no expert is named by more than 128 rows, and in some block some expert is named by exactly 128 rows.
All inputs are finite; a program needn't handle non-finite values.
Results may differ from the reference program's by a relative error of at most 0.0027.
Values may be sent and summed in bfloat16 or wider, within the bound.
A program may use at most 64 MiB of HBM per device.

```python
import math
import jax
import jax.numpy as jnp
import numpy as np
from jax import lax

D = 2048
HW = 512
T_DEV = 128
TOPK = 4
EXPERTS = 8
CAP = 128
ROWS_MEAN = 1024
TOKENS = 2048
N_DP = 2
N_EXPERT = 8


def shard_levels(stream_key, dims, cuts, least, top_value):
    loudness, own = 1.0, jax.random.fold_in(stream_key, 6)
    for axis_at, blocks in cuts:
        steps = jnp.exp(jax.random.uniform(jax.random.fold_in(own, axis_at), (blocks,), jnp.float32, least / len(cuts), top_value / len(cuts)))
        loudness = loudness * jnp.repeat(steps, dims[axis_at] // blocks).reshape([-1 if axis == axis_at else 1 for axis in range(len(dims))])
    return loudness


def assign_block(stream_key, own, number, rows, count, top, bound, skew):
    ranking = jax.random.permutation(stream_key, count)
    packed, usual = portions_of(count, rows * top, bound, skew, True), portions_of(count, rows * top, bound, skew, False)
    places = jnp.arange(count)

    def named(sizes, offset_by):
        used = int((sizes > 0).sum())
        fixed = max(1, used // 4)
        moved = fixed + (places - fixed + offset_by * (used - fixed)) % max(1, count - fixed)
        return jnp.zeros((count,), jnp.int32).at[ranking[jnp.where(places < fixed, places, moved)]].set(jnp.asarray(sizes, jnp.int32))

    sizes = jnp.where(number % 4 == 0, named(packed, number // 4), named(usual, number - number // 4 - 1))
    mixed = jax.random.permutation(jax.random.fold_in(own, 3), count)
    giver, receiver = mixed[0:count // 2 * 2:2], mixed[1:count // 2 * 2:2]
    room = jnp.minimum(sizes[giver] - 1, bound - sizes[receiver]) // 2
    room = jnp.where((giver == ranking[0]) | (receiver == ranking[0]) | (sizes[receiver] == 0), 0, jnp.maximum(room, 0))
    moved = jax.random.randint(jax.random.fold_in(own, 4), (count // 2,), 0, 1 << 20) % (room + 1)
    sizes = sizes.at[giver].add(-moved).at[receiver].add(moved)
    labels = jnp.searchsorted(jnp.cumsum(sizes), jnp.arange(rows * top), side="right").astype(jnp.int32)
    grid = labels.reshape(top, rows).T
    grid = grid[jax.random.permutation(jax.random.fold_in(own, 1), rows)]
    offset_by = jax.random.randint(jax.random.fold_in(own, 2), (rows, 1), 0, top)
    return jnp.take_along_axis(grid, (jnp.arange(top)[None, :] + offset_by) % top, axis=1)


def portions_of(amount, total, limit, slope, full):
    loads = [(1 << 20) // math.isqrt(grade ** slope) + 1 for grade in range(1, amount + 1)]
    largest = limit if full else min(limit, max(-(-total // amount), total * loads[0] // sum(loads)))
    least = 1 if total - largest >= amount - 1 else 0
    holding, spare = [largest] + [least] * (amount - 1), total - largest - least * (amount - 1)
    while spare > 0:
        candidates = [i for i in range(1, amount) if holding[i] < largest] or [i for i in range(1, amount) if holding[i] < limit]
        pool, budget = sum([loads[i] for i in candidates]), spare
        for i in candidates:
            addition = min(limit - holding[i], max(1, budget * loads[i] // pool), spare)
            holding[i] = holding[i] + addition
            spare = spare - addition
    return np.array(holding)


def scatter_about(own_key, shape, deviation, bound, pieces=(), kind=jnp.bfloat16):
    entries = jax.random.normal(own_key, shape, jnp.float32) * deviation
    if len(pieces) > 0:
        entries = shard_levels(own_key, shape, pieces, -0.22, 0.18) * entries
    return jnp.clip(entries, min=-bound, max=bound).astype(kind)


def setup_inputs(seed: int = 0, part: int = 0) -> dict:
    streams_of = jax.random.split(jax.random.key(seed), 5)
    part_splits = jax.random.split(jax.random.fold_in(streams_of[4], part), 5)
    tokens = scatter_about(part_splits[0], (TOKENS, D), 1.0, 6.0, ((0, 16),))
    routes_keys = jax.random.split(jax.random.fold_in(part_splits[1], 1), TOKENS // T_DEV)
    routes_turns = jax.random.permutation(jax.random.fold_in(part_splits[1], 3), TOKENS // T_DEV)
    routes = jax.vmap(lambda own, number: assign_block(jax.random.fold_in(part_splits[1], 2), own, number, T_DEV, EXPERTS, TOPK, CAP, 2))(routes_keys, routes_turns).reshape((TOKENS, TOPK))
    w_gate = scatter_about(part_splits[2], (EXPERTS, D, HW), D ** -0.5, 0.125, ((0, 8),))
    w_up = scatter_about(part_splits[3], (EXPERTS, D, HW), D ** -0.5, 0.125, ((0, 8),))
    return dict(tokens=tokens, routes=routes, w_gate=w_gate, w_up=w_up)


RIDGE = 0.05

def reference(tokens, routes, w_gate, w_up):
    row_limit = N_DP * N_EXPERT * CAP

    def per_expert(expert_id):
        member = jnp.any(routes == expert_id, axis=1)
        row_ids = jnp.nonzero(member, size=row_limit, fill_value=0)[0].astype(jnp.int32)
        valid = jnp.arange(row_limit, dtype=jnp.int32) < jnp.sum(member.astype(jnp.int32))
        picked = tokens[row_ids]
        gate_proj = jnp.dot(picked.astype(jnp.float32), w_gate[expert_id].astype(jnp.float32), preferred_element_type=jnp.float32)
        up_proj = jnp.dot(picked.astype(jnp.float32), w_up[expert_id].astype(jnp.float32), preferred_element_type=jnp.float32)
        hidden = jnp.where(valid[:, None], jax.nn.silu(gate_proj) * up_proj, 0.0).astype(jnp.bfloat16)
        gram_local = lax.dot_general(hidden.astype(jnp.float32), hidden.astype(jnp.float32), (((0,), (0,)), ((), ())), preferred_element_type=jnp.float32)
        regular = gram_local / ROWS_MEAN + RIDGE * jnp.eye(HW, dtype=jnp.float32)
        return jnp.linalg.cholesky(regular).T
    return lax.map(per_expert, jnp.arange(EXPERTS, dtype=jnp.int32))
```

```python
import functools

import jax
import jax.numpy as jnp
from jax import lax
from jax.experimental import pallas as pl
from jax.experimental.pallas import tpu as pltpu
from jax.sharding import PartitionSpec as P

RIDGE = 0.05
TILE = 128
SUB = 8
PIECES = 2
MESH = pl.DeviceIdType.MESH


def spread_lane(x, lane):
    return jnp.broadcast_to(x[:, lane : lane + 1], x.shape)


def factor_tile(tile):
    width = tile.shape[0]
    groups = width // SUB
    row_id = lax.broadcasted_iota(jnp.int32, (SUB, width), 0)
    col_id = lax.broadcasted_iota(jnp.int32, (SUB, width), 1)
    rest = [tile[SUB * k : SUB * k + SUB, :] for k in range(groups)]
    inverse = [(col_id == row_id + SUB * k).astype(jnp.float32) for k in range(groups)]
    factor_rows, inverse_rows = [], []
    for k in range(groups):
        p, q = rest[k], inverse[k]
        cols = [spread_lane(p, SUB * k + c) for c in range(SUB)]
        out_p, out_q = jnp.zeros_like(p), jnp.zeros_like(q)
        for i in range(SUB):
            pivot = cols[i][i : i + 1, :]
            inv, scale = 1.0 / pivot, lax.rsqrt(pivot)
            keep = row_id == i
            out_p = jnp.where(keep, p * scale, out_p)
            out_q = jnp.where(keep, q * scale, out_q)
            m = cols[i]

            def eliminate(x):
                u = x[i : i + 1, :] * inv
                return jnp.where(keep, u, x - m * u)

            for c in range(i + 1, SUB):
                cols[c] = eliminate(cols[c])
            p, q = eliminate(p), eliminate(q)
        factor_rows.append(jnp.where(col_id >= row_id + SUB * k, out_p, 0.0))
        inverse_rows.append(out_q)
        for kk in range(k + 1, groups):
            old = rest[kk]
            new, new_inverse = old, inverse[kk]
            for c in range(SUB):
                m = spread_lane(old, SUB * k + c)
                new = new - m * p[c : c + 1, :]
                new_inverse = new_inverse - m * q[c : c + 1, :]
            rest[kk], inverse[kk] = new, new_inverse
    return jnp.concatenate(factor_rows, 0), jnp.concatenate(inverse_rows, 0)


def cholesky_kernel(scale, rank_ref, gram_ref, out_ref, work, factor):
    size = gram_ref.shape[0]
    row = lax.broadcasted_iota(jnp.int32, (size, size), 0)
    col = lax.broadcasted_iota(jnp.int32, (size, size), 1)
    work[...] = gram_ref[...] * scale + jnp.where(row == col, RIDGE, 0.0)
    factor[...] = jnp.zeros_like(factor)
    for b in range(size // TILE):
        lo, hi = b * TILE, (b + 1) * TILE
        upper, lower = factor_tile(work[lo:hi, lo:hi])
        factor[lo:hi, lo:hi] = upper
        if hi < size:
            beside = jnp.dot(
                lower, work[lo:hi, hi:], preferred_element_type=jnp.float32,
                precision=lax.Precision.HIGHEST,
            )
            factor[lo:hi, hi:] = beside
            for r in range(hi, size, TILE):
                work[r : r + TILE, r:] -= lax.dot_general(
                    beside[:, r - hi : r - hi + TILE], beside[:, r - hi :],
                    (((0,), (0,)), ((), ())), preferred_element_type=jnp.float32,
                    precision=lax.Precision.HIGHEST,
                )
    rows = out_ref.shape[0]
    out_ref[...] = factor[pl.ds(pl.multiple_of(rank_ref[0] * rows, 8), rows), :]


def cholesky_rows(gram, rows_mean, my_rank, block_rows):
    size = gram.shape[0]
    return pl.pallas_call(
        functools.partial(cholesky_kernel, 1.0 / rows_mean),
        out_shape=jax.ShapeDtypeStruct((block_rows, size), jnp.float32),
        in_specs=[
            pl.BlockSpec(memory_space=pltpu.SMEM),
            pl.BlockSpec(memory_space=pltpu.VMEM),
        ],
        out_specs=pl.BlockSpec(memory_space=pltpu.VMEM),
        scratch_shapes=[
            pltpu.VMEM((size, size), jnp.float32),
            pltpu.VMEM((size, size), jnp.float32),
        ],
        compiler_params=pltpu.CompilerParams(vmem_limit_bytes=32 * 2**20),
        name="cholesky",
    )(my_rank.astype(jnp.int32).reshape(1), gram)


def gated(x, w_gate, w_up):
    gate = jnp.dot(x, w_gate, preferred_element_type=jnp.float32)
    up = jnp.dot(x, w_up, preferred_element_type=jnp.float32)
    return gate / (1.0 + jnp.exp(-gate)) * up


def gram_kernel(
    n, nd, tok_ref, mask_ref, wg_hbm, wu_hbm, gram_ref,
    tok, masks, hid, wg, wu,
    tok_recv, tok_send, share_recv, share_send, hid_recv, hid_send,
    mask_recv, mask_send, local_sem,
):
    chips = n // 2
    me = lax.axis_index("expert")
    my_dp = lax.axis_index("dp")
    z, core = me // 2, lax.rem(me, 2)
    sibling = z * 2 + (1 - core)
    rows = tok_ref.shape[0]
    piece = rows // PIECES

    weights = [
        pltpu.make_async_copy(wg_hbm, wg, local_sem.at[0]),
        pltpu.make_async_copy(wu_hbm, wu, local_sem.at[1]),
    ]
    for w in weights:
        w.start()
    own = [
        pltpu.make_async_copy(tok_ref, tok.at[me], local_sem.at[2]),
        pltpu.make_async_copy(mask_ref, masks.at[me], local_sem.at[3]),
    ]
    for o in own:
        o.start()

    barrier = pltpu.get_barrier_semaphore()
    for step in range(1, n):
        pl.semaphore_signal(
            barrier, inc=1, device_id={"expert": lax.rem(me + step, n)}, device_id_type=MESH
        )
    for step in range(1, nd):
        pl.semaphore_signal(
            barrier, inc=1, device_id={"dp": lax.rem(my_dp + step, nd)}, device_id_type=MESH
        )
    for o in own:
        o.wait()
    pl.semaphore_wait(barrier, n - 1 + nd - 1)

    def part(c):
        return pl.ds(c * piece, piece)

    def token_copy(slot_z, c, way):
        slot = slot_z * 2 + core
        to = me + 2 if way == 0 else me - 2
        return pltpu.make_async_remote_copy(
            src_ref=tok.at[slot, part(c)], dst_ref=tok.at[slot, part(c)],
            send_sem=tok_send.at[way, slot_z, c], recv_sem=tok_recv.at[slot_z, c],
            device_id={"expert": to}, device_id_type=MESH,
        )

    def share_copy(slot_z, c):
        slot = slot_z * 2 + core
        return pltpu.make_async_remote_copy(
            src_ref=tok.at[slot, part(c)], dst_ref=tok.at[slot, part(c)],
            send_sem=share_send.at[slot_z, c], recv_sem=share_recv.at[slot_z, c],
            device_id={"expert": sibling}, device_id_type=MESH,
        )

    def mask_copy(step):
        return pltpu.make_async_remote_copy(
            src_ref=mask_ref, dst_ref=masks.at[me],
            send_sem=mask_send.at[step], recv_sem=mask_recv.at[step],
            device_id={"expert": lax.rem(me + step, n)}, device_id_type=MESH,
        )

    def hidden_copy(slot_z, c, step):
        where = (my_dp, pl.ds(slot_z * 2, 2), part(c))
        return pltpu.make_async_remote_copy(
            src_ref=hid.at[where], dst_ref=hid.at[where],
            send_sem=hid_send.at[step - 1, slot_z, c], recv_sem=hid_recv.at[step - 1, slot_z, c],
            device_id={"dp": lax.rem(my_dp + step, nd)}, device_id_type=MESH,
        )

    for c in range(PIECES):
        @pl.when(z < chips - 1)
        def _():
            token_copy(z, c, 0).start()

        @pl.when(z > 0)
        def _():
            token_copy(z, c, 1).start()

        share_copy(z, c).start()
    for step in range(1, n):
        mask_copy(step).start()
    for step in range(1, n):
        mask_copy(step).wait_recv()
    for w in weights:
        w.wait()

    eye = lax.broadcasted_iota(jnp.int32, (rows, rows), 0) == lax.broadcasted_iota(
        jnp.int32, (rows, rows), 1
    )

    def mask_column(slot):
        line = masks[slot, pl.ds(me, 1), :]
        return jnp.sum(jnp.where(eye, line, 0.0), axis=1, keepdims=True)

    def experts_of(slot_z, c):
        x = tok[pl.ds(slot_z * 2, 2), part(c), :].reshape(2 * piece, -1)
        keep = jnp.concatenate(
            [mask_column(slot_z * 2 + k)[c * piece : (c + 1) * piece] for k in range(2)], 0
        )
        h = jnp.where(keep > 0.0, gated(x, wg[...], wu[...]), 0.0).astype(jnp.bfloat16)
        hid[my_dp, pl.ds(slot_z * 2, 2), part(c), :] = h.reshape(2, piece, -1)
        for step in range(1, nd):
            hidden_copy(slot_z, c, step).start()

    def add_gram(slot_z, first=False):
        for c in range(PIECES):
            for step in range(1, nd):
                hidden_copy(slot_z, c, step).wait_recv()
        h = hid[:, pl.ds(slot_z * 2, 2)].reshape(nd * 2 * rows, -1)
        g = lax.dot_general(h, h, (((0,), (0,)), ((), ())), preferred_element_type=jnp.float32)
        gram_ref[...] = g if first else gram_ref[...] + g

    for c in range(PIECES):
        share_copy(z, c).wait_recv()
        experts_of(z, c)

    for hop in range(1, chips):
        for c in range(PIECES):
            for way in range(2):
                slot_z = z - hop if way == 0 else z + hop

                @pl.when(slot_z >= 0 if way == 0 else slot_z < chips)
                def _():
                    token_copy(slot_z, c, way).wait_recv()

                    @pl.when(z < chips - 1 if way == 0 else z > 0)
                    def _():
                        token_copy(slot_z, c, way).start()

                    share_copy(slot_z, c).start()
                    share_copy(slot_z, c).wait_recv()
                    experts_of(slot_z, c)
        if hop == 1:
            add_gram(z, first=True)
        else:
            for way in range(2):
                slot_z = z - hop + 1 if way == 0 else z + hop - 1

                @pl.when(slot_z >= 0 if way == 0 else slot_z < chips)
                def _():
                    add_gram(slot_z)
    for way in range(2):
        slot_z = z - chips + 1 if way == 0 else z + chips - 1

        @pl.when(slot_z >= 0 if way == 0 else slot_z < chips)
        def _():
            add_gram(slot_z)

    for step in range(1, n):
        mask_copy(step).wait_send()
    for slot_z in range(chips):
        for c in range(PIECES):
            @pl.when((z < chips - 1) & (slot_z <= z))
            def _():
                token_copy(slot_z, c, 0).wait_send()

            @pl.when((z > 0) & (slot_z >= z))
            def _():
                token_copy(slot_z, c, 1).wait_send()

            share_copy(slot_z, c).wait_send()
            for step in range(1, nd):
                hidden_copy(slot_z, c, step).wait_send()


def gathered_gram(tokens, mask, w_gate, w_up, n, nd):
    rows, depth = tokens.shape
    width = w_gate.shape[1]
    chips = n // 2
    dma = pltpu.SemaphoreType.DMA
    return pl.pallas_call(
        functools.partial(gram_kernel, n, nd),
        out_shape=jax.ShapeDtypeStruct((width, width), jnp.float32),
        in_specs=[
            pl.BlockSpec(memory_space=pltpu.VMEM),
            pl.BlockSpec(memory_space=pltpu.VMEM),
            pl.BlockSpec(memory_space=pl.ANY),
            pl.BlockSpec(memory_space=pl.ANY),
        ],
        out_specs=pl.BlockSpec(memory_space=pltpu.VMEM),
        scratch_shapes=[
            pltpu.VMEM((n, rows, depth), jnp.bfloat16),
            pltpu.VMEM((n,) + mask.shape, jnp.float32),
            pltpu.VMEM((nd, n, rows, width), jnp.bfloat16),
            pltpu.VMEM((depth, width), jnp.bfloat16),
            pltpu.VMEM((depth, width), jnp.bfloat16),
            dma((chips, PIECES)),
            dma((2, chips, PIECES)),
            dma((chips, PIECES)),
            dma((chips, PIECES)),
            dma((max(nd - 1, 1), chips, PIECES)),
            dma((max(nd - 1, 1), chips, PIECES)),
            dma((n,)),
            dma((n,)),
            dma((4,)),
        ],
        compiler_params=pltpu.CompilerParams(
            collective_id=0, has_side_effects=True, vmem_limit_bytes=48 * 2**20
        ),
        name="gathered_gram",
    )(tokens, mask, w_gate, w_up)


def routed_gram(tokens, routes, w_gate, w_up, experts, capacity):
    tok_rows = routes.shape[0]
    model_width = tokens.shape[1]
    ids = jnp.arange(experts, dtype=jnp.int32)
    member = jnp.any(routes[:, :, None] == ids, axis=1)
    earlier = jnp.tril(jnp.ones((tok_rows, tok_rows), jnp.float32), -1)
    position = jnp.dot(earlier, member.astype(jnp.float32)).astype(jnp.int32)
    slots = jnp.arange(capacity, dtype=jnp.int32)[None, :, None]
    chosen = member.T[:, None, :] & (position.T[:, None, :] == slots)
    outbox = jnp.dot(
        chosen.reshape(-1, tok_rows).astype(tokens.dtype), tokens,
        preferred_element_type=jnp.float32,
    ).astype(tokens.dtype)
    outbox = outbox.reshape(experts, capacity, model_width)
    arrived = lax.all_to_all(outbox, "expert", split_axis=0, concat_axis=0, tiled=True)
    hidden = gated(arrived.reshape(-1, model_width), w_gate, w_up).astype(jnp.bfloat16)
    gram = lax.dot_general(
        hidden, hidden, (((0,), (0,)), ((), ())), preferred_element_type=jnp.float32
    )
    return lax.psum(gram, "dp")


def body(tokens, routes, w_gate, w_up):
    owners = lax.axis_size("expert")
    data_ranks = lax.axis_size("dp")
    experts = w_gate.shape[0] * owners
    factor_width = w_gate.shape[2]
    tok_rows, top_count = routes.shape
    capacity = min(tok_rows, 2 * tok_rows * top_count // experts)
    if capacity == tok_rows and owners % 2 == 0:
        ids = jnp.arange(-(-experts // 8) * 8, dtype=jnp.int32)
        mask = jnp.any(routes.T[None] == ids[:, None, None], axis=1).astype(jnp.float32)
        gram = gathered_gram(tokens, mask, w_gate[0], w_up[0], owners, data_ranks)
    else:
        gram = routed_gram(tokens, routes, w_gate[0], w_up[0], experts, capacity)
    rows_mean = data_ranks * tok_rows * top_count
    block_rows = factor_width // data_ranks
    my_rows = cholesky_rows(gram, rows_mean, lax.axis_index("dp"), block_rows)
    return my_rows.reshape(1, block_rows, factor_width)


def solution(mesh):
    in_specs = (
        P(("groups", "dp", "expert"), None),
        P(("groups", "dp", "expert"), None),
        P(("groups", "expert"), None, None),
        P(("groups", "expert"), None, None),
    )
    out_specs = P(("groups", "expert"), "dp", None)
    return jax.shard_map(body, mesh=mesh, in_specs=in_specs, out_specs=out_specs, check_vma=False)
```

```python
import functools

import jax
import jax.numpy as jnp
from jax import lax
from jax.experimental import pallas as pl
from jax.experimental.pallas import tpu as pltpu
from jax.sharding import PartitionSpec as P

RIDGE = 0.05
TILE = 128
SUB = 8
PIECES = 2
TOGETHER = 1
MESH = pl.DeviceIdType.MESH


def spread_lane(x, lane):
    return jnp.broadcast_to(x[:, lane : lane + 1], x.shape)


def factor_tile(tile):
    width = tile.shape[0]
    groups = width // SUB
    row_id = lax.broadcasted_iota(jnp.int32, (SUB, width), 0)
    col_id = lax.broadcasted_iota(jnp.int32, (SUB, width), 1)
    rest = [tile[SUB * k : SUB * k + SUB, :] for k in range(groups)]
    inverse = [(col_id == row_id + SUB * k).astype(jnp.float32) for k in range(groups)]
    factor_rows, inverse_rows = [], []
    for k in range(groups):
        p, q = rest[k], inverse[k]
        cols = [spread_lane(p, SUB * k + c) for c in range(SUB)]
        out_p, out_q = jnp.zeros_like(p), jnp.zeros_like(q)
        for i in range(SUB):
            pivot = cols[i][i : i + 1, :]
            inv, scale = 1.0 / pivot, lax.rsqrt(pivot)
            keep = row_id == i
            out_p = jnp.where(keep, p * scale, out_p)
            out_q = jnp.where(keep, q * scale, out_q)
            m = cols[i]

            def eliminate(x):
                u = x[i : i + 1, :] * inv
                return jnp.where(keep, u, x - m * u)

            for c in range(i + 1, SUB):
                cols[c] = eliminate(cols[c])
            p, q = eliminate(p), eliminate(q)
        factor_rows.append(jnp.where(col_id >= row_id + SUB * k, out_p, 0.0))
        inverse_rows.append(out_q)
        for kk in range(k + 1, groups):
            old = rest[kk]
            new, new_inverse = old, inverse[kk]
            for c in range(SUB):
                m = spread_lane(old, SUB * k + c)
                new = new - m * p[c : c + 1, :]
                new_inverse = new_inverse - m * q[c : c + 1, :]
            rest[kk], inverse[kk] = new, new_inverse
    return jnp.concatenate(factor_rows, 0), jnp.concatenate(inverse_rows, 0)


def cholesky_kernel(scale, rank_ref, gram_ref, out_ref, work, factor):
    size = gram_ref.shape[0]
    row = lax.broadcasted_iota(jnp.int32, (size, size), 0)
    col = lax.broadcasted_iota(jnp.int32, (size, size), 1)
    work[...] = gram_ref[...] * scale + jnp.where(row == col, RIDGE, 0.0)
    factor[...] = jnp.zeros_like(factor)
    for b in range(size // TILE):
        lo, hi = b * TILE, (b + 1) * TILE
        upper, lower = factor_tile(work[lo:hi, lo:hi])
        factor[lo:hi, lo:hi] = upper
        if hi < size:
            beside = jnp.dot(
                lower, work[lo:hi, hi:], preferred_element_type=jnp.float32,
                precision=lax.Precision.HIGHEST,
            )
            factor[lo:hi, hi:] = beside
            for r in range(hi, size, TILE):
                work[r : r + TILE, r:] -= lax.dot_general(
                    beside[:, r - hi : r - hi + TILE], beside[:, r - hi :],
                    (((0,), (0,)), ((), ())), preferred_element_type=jnp.float32,
                    precision=lax.Precision.HIGHEST,
                )
    rows = out_ref.shape[0]
    out_ref[...] = factor[pl.ds(pl.multiple_of(rank_ref[0] * rows, 8), rows), :]


def cholesky_rows(gram, rows_mean, my_rank, block_rows):
    size = gram.shape[0]
    return pl.pallas_call(
        functools.partial(cholesky_kernel, 1.0 / rows_mean),
        out_shape=jax.ShapeDtypeStruct((block_rows, size), jnp.float32),
        in_specs=[
            pl.BlockSpec(memory_space=pltpu.SMEM),
            pl.BlockSpec(memory_space=pltpu.VMEM),
        ],
        out_specs=pl.BlockSpec(memory_space=pltpu.VMEM),
        scratch_shapes=[
            pltpu.VMEM((size, size), jnp.float32),
            pltpu.VMEM((size, size), jnp.float32),
        ],
        compiler_params=pltpu.CompilerParams(vmem_limit_bytes=32 * 2**20),
        name="cholesky",
    )(my_rank.astype(jnp.int32).reshape(1), gram)


def gated(x, w_gate, w_up):
    gate = jnp.dot(x, w_gate, preferred_element_type=jnp.float32)
    up = jnp.dot(x, w_up, preferred_element_type=jnp.float32)
    return gate / (1.0 + jnp.exp(-gate)) * up


def gram_kernel(
    n, nd, tok_ref, mask_ref, wg_hbm, wu_hbm, gram_ref,
    tok, masks, hid, wg, wu,
    tok_recv, tok_send, share_recv, share_send, hid_recv, hid_send,
    mask_recv, mask_send, local_sem,
):
    chips = n // 2
    me = lax.axis_index("expert")
    my_dp = lax.axis_index("dp")
    z, core = me // 2, lax.rem(me, 2)
    sibling = z * 2 + (1 - core)
    rows = tok_ref.shape[0]
    piece = rows // PIECES

    weights = [
        pltpu.make_async_copy(wg_hbm, wg, local_sem.at[0]),
        pltpu.make_async_copy(wu_hbm, wu, local_sem.at[1]),
    ]
    for w in weights:
        w.start()
    own = [
        pltpu.make_async_copy(tok_ref, tok.at[me], local_sem.at[2]),
        pltpu.make_async_copy(mask_ref, masks.at[me], local_sem.at[3]),
    ]
    for o in own:
        o.start()

    barrier = pltpu.get_barrier_semaphore()
    for step in range(1, n):
        pl.semaphore_signal(
            barrier, inc=1, device_id={"expert": lax.rem(me + step, n)}, device_id_type=MESH
        )
    for step in range(1, nd):
        pl.semaphore_signal(
            barrier, inc=1, device_id={"dp": lax.rem(my_dp + step, nd)}, device_id_type=MESH
        )
    for o in own:
        o.wait()
    pl.semaphore_wait(barrier, n - 1 + nd - 1)

    def part(c, count=1):
        return pl.ds(c * piece, count * piece)

    def token_copy(slot_z, c, way):
        slot = slot_z * 2 + core
        to = me + 2 if way == 0 else me - 2
        return pltpu.make_async_remote_copy(
            src_ref=tok.at[slot, part(c)], dst_ref=tok.at[slot, part(c)],
            send_sem=tok_send.at[way, slot_z, c], recv_sem=tok_recv.at[slot_z, c],
            device_id={"expert": to}, device_id_type=MESH,
        )

    def share_copy(slot_z, c):
        slot = slot_z * 2 + core
        return pltpu.make_async_remote_copy(
            src_ref=tok.at[slot, part(c)], dst_ref=tok.at[slot, part(c)],
            send_sem=share_send.at[slot_z, c], recv_sem=share_recv.at[slot_z, c],
            device_id={"expert": sibling}, device_id_type=MESH,
        )

    def mask_copy(step):
        return pltpu.make_async_remote_copy(
            src_ref=mask_ref, dst_ref=masks.at[me],
            send_sem=mask_send.at[step], recv_sem=mask_recv.at[step],
            device_id={"expert": lax.rem(me + step, n)}, device_id_type=MESH,
        )

    def hidden_copy(slot_z, c, step):
        where = (my_dp, pl.ds(slot_z * 2, 2), part(c, TOGETHER))
        return pltpu.make_async_remote_copy(
            src_ref=hid.at[where], dst_ref=hid.at[where],
            send_sem=hid_send.at[step - 1, slot_z, c], recv_sem=hid_recv.at[step - 1, slot_z, c],
            device_id={"dp": lax.rem(my_dp + step, nd)}, device_id_type=MESH,
        )

    for c in range(PIECES):
        @pl.when(z < chips - 1)
        def _():
            token_copy(z, c, 0).start()

        @pl.when(z > 0)
        def _():
            token_copy(z, c, 1).start()

        share_copy(z, c).start()
    for step in range(1, n):
        mask_copy(step).start()
    for step in range(1, n):
        mask_copy(step).wait_recv()
    for w in weights:
        w.wait()

    eye = lax.broadcasted_iota(jnp.int32, (rows, rows), 0) == lax.broadcasted_iota(
        jnp.int32, (rows, rows), 1
    )

    def mask_column(slot):
        line = masks[slot, pl.ds(me, 1), :]
        return jnp.sum(jnp.where(eye, line, 0.0), axis=1, keepdims=True)

    def experts_of(slot_z, c):
        span = TOGETHER * piece
        x = tok[pl.ds(slot_z * 2, 2), part(c, TOGETHER), :].reshape(2 * span, -1)
        keep = jnp.concatenate(
            [mask_column(slot_z * 2 + k)[c * piece : c * piece + span] for k in range(2)], 0
        )
        h = jnp.where(keep > 0.0, gated(x, wg[...], wu[...]), 0.0).astype(jnp.bfloat16)
        hid[my_dp, pl.ds(slot_z * 2, 2), part(c, TOGETHER), :] = h.reshape(2, span, -1)
        for step in range(1, nd):
            hidden_copy(slot_z, c, step).start()

    def add_gram(slot_z, first=False):
        for c in range(0, PIECES, TOGETHER):
            for step in range(1, nd):
                hidden_copy(slot_z, c, step).wait_recv()
        h = hid[:, pl.ds(slot_z * 2, 2)].reshape(nd * 2 * rows, -1)
        g = lax.dot_general(h, h, (((0,), (0,)), ((), ())), preferred_element_type=jnp.float32)
        gram_ref[...] = g if first else gram_ref[...] + g

    for c in range(PIECES):
        share_copy(z, c).wait_recv()
        if (c + 1) % TOGETHER == 0:
            experts_of(z, c + 1 - TOGETHER)

    for hop in range(1, chips):
        for c in range(PIECES):
            for way in range(2):
                slot_z = z - hop if way == 0 else z + hop

                @pl.when(slot_z >= 0 if way == 0 else slot_z < chips)
                def _():
                    token_copy(slot_z, c, way).wait_recv()

                    @pl.when(z < chips - 1 if way == 0 else z > 0)
                    def _():
                        token_copy(slot_z, c, way).start()

                    share_copy(slot_z, c).start()

            if (c + 1) % TOGETHER == 0:
                for way in range(2):
                    slot_z = z - hop if way == 0 else z + hop

                    @pl.when(slot_z >= 0 if way == 0 else slot_z < chips)
                    def _():
                        for k in range(c + 1 - TOGETHER, c + 1):
                            share_copy(slot_z, k).wait_recv()
                        experts_of(slot_z, c + 1 - TOGETHER)
        if hop == 1:
            add_gram(z, first=True)
        else:
            for way in range(2):
                slot_z = z - hop + 1 if way == 0 else z + hop - 1

                @pl.when(slot_z >= 0 if way == 0 else slot_z < chips)
                def _():
                    add_gram(slot_z)
    for way in range(2):
        slot_z = z - chips + 1 if way == 0 else z + chips - 1

        @pl.when(slot_z >= 0 if way == 0 else slot_z < chips)
        def _():
            add_gram(slot_z)

    for step in range(1, n):
        mask_copy(step).wait_send()
    for slot_z in range(chips):
        for c in range(PIECES):
            @pl.when((z < chips - 1) & (slot_z <= z))
            def _():
                token_copy(slot_z, c, 0).wait_send()

            @pl.when((z > 0) & (slot_z >= z))
            def _():
                token_copy(slot_z, c, 1).wait_send()

            share_copy(slot_z, c).wait_send()
            if c % TOGETHER == 0:
                for step in range(1, nd):
                    hidden_copy(slot_z, c, step).wait_send()


def gathered_gram(tokens, mask, w_gate, w_up, n, nd):
    rows, depth = tokens.shape
    width = w_gate.shape[1]
    chips = n // 2
    dma = pltpu.SemaphoreType.DMA
    return pl.pallas_call(
        functools.partial(gram_kernel, n, nd),
        out_shape=jax.ShapeDtypeStruct((width, width), jnp.float32),
        in_specs=[
            pl.BlockSpec(memory_space=pltpu.HBM),
            pl.BlockSpec(memory_space=pltpu.VMEM),
            pl.BlockSpec(memory_space=pltpu.HBM),
            pl.BlockSpec(memory_space=pltpu.HBM),
        ],
        out_specs=pl.BlockSpec(memory_space=pltpu.VMEM),
        scratch_shapes=[
            pltpu.VMEM((n, rows, depth), jnp.bfloat16),
            pltpu.VMEM((n,) + mask.shape, jnp.float32),
            pltpu.VMEM((nd, n, rows, width), jnp.bfloat16),
            pltpu.VMEM((depth, width), jnp.bfloat16),
            pltpu.VMEM((depth, width), jnp.bfloat16),
            dma((chips, PIECES)),
            dma((2, chips, PIECES)),
            dma((chips, PIECES)),
            dma((chips, PIECES)),
            dma((max(nd - 1, 1), chips, PIECES)),
            dma((max(nd - 1, 1), chips, PIECES)),
            dma((n,)),
            dma((n,)),
            dma((4,)),
        ],
        compiler_params=pltpu.CompilerParams(
            collective_id=0, has_side_effects=True, vmem_limit_bytes=48 * 2**20
        ),
        name="gathered_gram",
    )(tokens, mask, w_gate, w_up)


def routed_gram(tokens, routes, w_gate, w_up, experts, capacity):
    tok_rows = routes.shape[0]
    model_width = tokens.shape[1]
    ids = jnp.arange(experts, dtype=jnp.int32)
    member = jnp.any(routes[:, :, None] == ids, axis=1)
    earlier = jnp.tril(jnp.ones((tok_rows, tok_rows), jnp.float32), -1)
    position = jnp.dot(earlier, member.astype(jnp.float32)).astype(jnp.int32)
    slots = jnp.arange(capacity, dtype=jnp.int32)[None, :, None]
    chosen = member.T[:, None, :] & (position.T[:, None, :] == slots)
    outbox = jnp.dot(
        chosen.reshape(-1, tok_rows).astype(tokens.dtype), tokens,
        preferred_element_type=jnp.float32,
    ).astype(tokens.dtype)
    outbox = outbox.reshape(experts, capacity, model_width)
    arrived = lax.all_to_all(outbox, "expert", split_axis=0, concat_axis=0, tiled=True)
    hidden = gated(arrived.reshape(-1, model_width), w_gate, w_up).astype(jnp.bfloat16)
    gram = lax.dot_general(
        hidden, hidden, (((0,), (0,)), ((), ())), preferred_element_type=jnp.float32
    )
    return lax.psum(gram, "dp")


def body(tokens, routes, w_gate, w_up):
    owners = lax.axis_size("expert")
    data_ranks = lax.axis_size("dp")
    experts = w_gate.shape[0] * owners
    factor_width = w_gate.shape[2]
    tok_rows, top_count = routes.shape
    capacity = min(tok_rows, 2 * tok_rows * top_count // experts)
    if capacity == tok_rows and owners % 2 == 0:
        ids = jnp.arange(-(-experts // 8) * 8, dtype=jnp.int32)
        mask = jnp.any(routes.T[None] == ids[:, None, None], axis=1).astype(jnp.float32)
        gram = gathered_gram(tokens, mask, w_gate[0], w_up[0], owners, data_ranks)
    else:
        gram = routed_gram(tokens, routes, w_gate[0], w_up[0], experts, capacity)
    rows_mean = data_ranks * tok_rows * top_count
    block_rows = factor_width // data_ranks
    my_rows = cholesky_rows(gram, rows_mean, lax.axis_index("dp"), block_rows)
    return my_rows.reshape(1, block_rows, factor_width)


def solution(mesh):
    in_specs = (
        P(("groups", "dp", "expert"), None),
        P(("groups", "dp", "expert"), None),
        P(("groups", "expert"), None, None),
        P(("groups", "expert"), None, None),
    )
    out_specs = P(("groups", "expert"), "dp", None)
    return jax.shard_map(body, mesh=mesh, in_specs=in_specs, out_specs=out_specs, check_vma=False)
```
